512 devices in a mesh: band: 256 (over z, x_hi, y, core), grid: 2 (over x_lo).
Axes of the slice: x: 4 (x_hi: 2, x_lo: 2; x = x_hi * 2 + x_lo), y: 8, z: 8, core: 2. Of those that a mesh axis runs over, the one named last changes fastest.
Arguments:
- orbitals: float32 [512, 64, 4096], P('band', 'grid'), may hold values from -4 to 4
- pair_list: int32 [256, 4, 2], P('band'), may hold values from 0 to 511, as said below
- pair_count: int32 [256], P('band'), may hold values from 1 to 4, 512 in all
Outputs:
- exchange_proj: float32 [512, 64, 4096], P('band', 'grid')
The draws below stay inside these ranges and needn't reach their ends.
Inputs may be any that keep to these rules, and one draw needn't show every extreme that they name: `pair_list`: entry 0 is an orbital index 0 to 1 within the row's band group; entry 1 is a global orbital index owned by the same band group or by one of the next 2 groups, counted cyclically; the two never name the same orbital. Band group b uses its first pair_count[b] slots.
All inputs are finite; a program needn't handle non-finite values.
Results may differ from the reference program's by a relative error of at most 0.0003.
Values sent between devices are 32-bit elements; how exact they have to be, the bound alone decides.
No kernel may reach another device: no remote copies, remote signals or barrier semaphores. Data moves between devices by JAX's collectives and lax.ppermute only.
A program may use at most 64 MiB of HBM per device.

```python
import math
import jax
import jax.numpy as jnp
import numpy as np
from jax import lax

CELL_SPAN_COUNT = 64
ORB_DEV = 2
PAIR_MEAN = 2
REACH = 2
SLOTS = 4
NORB = 512
N_BAND = 256


def draw_orbitals(key, part):
    lattice_position = jnp.arange(CELL_SPAN_COUNT).astype(jnp.float32)
    spread = CELL_SPAN_COUNT / 4.0

    def single(number):
        folded = jax.random.fold_in(jax.random.fold_in(key, 7001), number)
        key_centre, key_wave, key_phase, key_rough = jax.random.split(folded, 4)
        centre = jax.random.uniform(key_centre, (3,), minval=0.0, maxval=float(CELL_SPAN_COUNT))
        offsets = jnp.abs(lattice_position[None, :] - centre[:, None])
        offsets = jnp.minimum(offsets, CELL_SPAN_COUNT - offsets)
        radius = offsets[0][:, None, None] ** 2 + offsets[1][None, :, None] ** 2 + offsets[2][None, None, :] ** 2
        bell_shaped_decay = jnp.exp(-radius / (2.0 * spread * spread))
        fourier_modes = jax.random.randint(key_wave, (3,), 2, CELL_SPAN_COUNT * 5 // 16 + 1).astype(jnp.float32)
        angular_displacements = jax.random.uniform(key_phase, (3,), minval=0.0, maxval=2.0 * math.pi)
        oscillating_sinusoids = jnp.cos(fourier_modes[:, None] * lattice_position[None, :] * (2.0 * math.pi / CELL_SPAN_COUNT) + angular_displacements[:, None])
        oscillating_sinusoid = oscillating_sinusoids[0][:, None, None] * oscillating_sinusoids[1][None, :, None] * oscillating_sinusoids[2][None, None, :]
        random_perturbation = jnp.clip(0.5 * jax.random.normal(key_rough, (CELL_SPAN_COUNT, CELL_SPAN_COUNT, CELL_SPAN_COUNT)), -0.9, 0.9)
        electron_function_samples = jnp.clip(2.5 * bell_shaped_decay * (oscillating_sinusoid + 0.45 * random_perturbation), -4.0, 4.0)
        return electron_function_samples.reshape(CELL_SPAN_COUNT, CELL_SPAN_COUNT * CELL_SPAN_COUNT).astype(jnp.float32)
    return lax.map(single, jnp.arange(NORB))


def draw_pair_list(key, part):
    groups = NORB // ORB_DEV
    key_first, key_hop, key_partner = jax.random.split(jax.random.fold_in(key, 7002), 3)
    first_index = jax.random.randint(key_first, (groups, SLOTS), 0, ORB_DEV)
    hop_count = jax.random.randint(key_hop, (groups, SLOTS), 0, REACH + 1)
    partner = jax.random.randint(key_partner, (groups, SLOTS), 0, ORB_DEV)
    partner = jnp.where((hop_count == 0) & (partner == first_index), (first_index + 1) % ORB_DEV, partner)
    group_ids = jnp.arange(groups, dtype=jnp.int32)[:, None]
    global_partner = (group_ids + hop_count) % groups * ORB_DEV + partner
    return jnp.stack([first_index, global_partner], axis=-1).astype(jnp.int32)


def split_up(amount, total, bound, slope):
    portions = [(1 << 20) // math.isqrt(standing ** slope) + 1 for standing in range(2, amount + 1)]
    surplus, given = total - bound - (amount - 1), [1] * (amount - 1)
    while surplus > 0:
        movable = [i for i in range(amount - 1) if given[i] < bound]
        mass, budget = sum([portions[i] for i in movable]), surplus
        for i in movable:
            addition = min(bound - given[i], max(1, budget * portions[i] // mass), surplus)
            given[i] = given[i] + addition
            surplus = surplus - addition
    return np.array([bound] + given)


def ragged_sizes(own_key, count, total, reach, skew):
    if count == 2:
        one = jax.random.randint(own_key, (), max(1, total - reach), min(reach, total - 1) + 1)
        return jnp.stack([one, total - one])
    sizes = jnp.asarray(split_up(count, total, reach, skew), jnp.int32)
    pairs = (count - 1) // 2
    source_of, receiver = sizes[1:1 + 2 * pairs:2], sizes[2:2 + 2 * pairs:2]
    margin = jnp.minimum(source_of - 1, reach - receiver)
    shifted = jax.random.randint(jax.random.fold_in(own_key, 1), (pairs,), 0, 1 << 20) % (margin + 1)
    sizes = sizes.at[1:1 + 2 * pairs:2].set(source_of - shifted).at[2:2 + 2 * pairs:2].set(receiver + shifted)
    return sizes[jax.random.permutation(jax.random.fold_in(own_key, 2), count)]


def setup_inputs(seed: int = 0) -> dict:
    key_of = jax.random.split(jax.random.key(seed), 4)
    return {
        "orbitals": draw_orbitals(jax.random.fold_in(key_of[3], 71), 0),
        "pair_list": draw_pair_list(jax.random.fold_in(key_of[3], 71), 0),
        "pair_count": ragged_sizes(key_of[2], N_BAND, PAIR_MEAN * N_BAND, SLOTS, 2).astype(jnp.int32),
    }


def kernel_table():
    points = jnp.arange(CELL_SPAN_COUNT).astype(jnp.float32)
    eigenvalues = 2.0 - 2.0 * jnp.cos(points * (2.0 * math.pi / CELL_SPAN_COUNT))
    summed = eigenvalues[:, None, None] + eigenvalues[None, :, None] + eigenvalues[None, None, :]
    return (1.0 / CELL_SPAN_COUNT) / (1.0 / CELL_SPAN_COUNT ** 2 + summed)


def reference(orbitals, pair_list, pair_count):
    groups = pair_list.shape[0]
    slot_count = pair_list.shape[1]
    kernel = kernel_table()
    group_ids = jnp.repeat(jnp.arange(groups, dtype=jnp.int32), slot_count)
    flat = pair_list.reshape(-1, 2).astype(jnp.int32)
    first_index = (group_ids * ORB_DEV + flat[:, 0]).astype(jnp.int32)
    second = flat[:, 1].astype(jnp.int32)
    alive = (jnp.arange(slot_count)[None, :] < pair_count[:, None]).reshape(-1).astype(orbitals.dtype)

    def visit(totals, inputs):
        left_id, right_id, weight = inputs
        left_rows = orbitals[left_id]
        right_rows = orbitals[right_id]
        density = (left_rows * right_rows * weight).reshape(CELL_SPAN_COUNT, CELL_SPAN_COUNT, CELL_SPAN_COUNT)
        spectrum = jnp.fft.fftn(density) * kernel
        potential = jnp.real(jnp.fft.ifftn(spectrum)).astype(density.dtype).reshape(CELL_SPAN_COUNT, CELL_SPAN_COUNT * CELL_SPAN_COUNT)
        totals = totals.at[left_id].add(potential * right_rows)
        totals = totals.at[right_id].add(potential * left_rows)
        return totals, None

    totals, unused = lax.scan(visit, jnp.zeros(orbitals.shape, orbitals.dtype), (first_index, second, alive))
    return totals
```

```python
import functools
import math

import jax
import jax.numpy as jnp
import ml_dtypes
import numpy as np
from jax import lax
from jax.experimental import pallas as pl
from jax.experimental.pallas import tpu as pltpu
from jax.sharding import PartitionSpec as P

SIDE = 64
TILES = SIDE // 2
LANES = 2 * SIDE
CHUNKS = 1


class Factors:
    def __init__(self, fetch, swap):
        self.fetch = fetch
        self.swap = swap


def turn(re, im, c, s):
    return re * c + im * s, im * c - re * s


def turn_back(re, im, c, s):
    return re * c - im * s, im * c + re * s


def complex_forward(re, im, size, factors):
    tiles = size // 2
    if tiles == 1:
        return [re[0], im[0]]
    half = tiles // 2
    even_re = [re[t] + re[t + half] for t in range(half)]
    even_im = [im[t] + im[t + half] for t in range(half)]
    odd_re, odd_im = [], []
    for t in range(half):
        a, b = re[t] - re[t + half], im[t] - im[t + half]
        if size == 4:
            a, b = factors.swap(a, b), factors.swap(b, -a)
        else:
            a, b = turn(a, b, *factors.fetch(size, t))
        odd_re.append(a)
        odd_im.append(b)
    return complex_forward(even_re, even_im, size // 2, factors) + complex_forward(
        odd_re, odd_im, size // 2, factors
    )


def complex_back(parts, size, factors):
    tiles = size // 2
    if tiles == 1:
        return [parts[0]], [parts[1]]
    half = tiles // 2
    even_re, even_im = complex_back(parts[:tiles], size // 2, factors)
    odd_re, odd_im = complex_back(parts[tiles:], size // 2, factors)
    low_re, low_im, high_re, high_im = [], [], [], []
    for t in range(half):
        a, b = odd_re[t], odd_im[t]
        if size == 4:
            a, b = factors.swap(a, -b), factors.swap(b, a)
        else:
            a, b = turn_back(a, b, *factors.fetch(size, t))
        low_re.append(even_re[t] + a)
        low_im.append(even_im[t] + b)
        high_re.append(even_re[t] - a)
        high_im.append(even_im[t] - b)
    return low_re + high_re, low_im + high_im


def real_forward(values, size, factors):
    tiles = size // 2
    if tiles == 1:
        return list(values)
    half = tiles // 2
    sums = [values[t] + values[t + half] for t in range(half)]
    rests = [values[t] - values[t + half] for t in range(half)]
    if size == 4:
        odd = rests
    else:
        quarter = half // 2
        re, im = [], []
        for t in range(quarter):
            a, b = turn(rests[t], -rests[t + quarter], *factors.fetch(size, t))
            re.append(a)
            im.append(b)
        odd = complex_forward(re, im, size // 4, factors)
    return real_forward(sums, size // 2, factors) + odd


def real_back(parts, size, factors):
    tiles = size // 2
    if tiles == 1:
        return list(parts)
    half = tiles // 2
    sums = real_back(parts[:half], size // 2, factors)
    if size == 4:
        rests = parts[half:]
    else:
        re, im = complex_back(parts[half:], size // 4, factors)
        quarter = half // 2
        low, high = [], []
        for t in range(quarter):
            a, b = turn_back(re[t], im[t], *factors.fetch(size, t))
            low.append(a)
            high.append(-b)
        rests = low + high
    return [sums[t] + rests[t] for t in range(half)] + [sums[t] - rests[t] for t in range(half)]


def factor_rows():
    rows, place, wanted = [], {}, []

    def note(size, t):
        if (size, t) not in wanted:
            wanted.append((size, t))
        angle = 2.0 * math.pi * (2 * t + np.arange(2)) / size
        return np.cos(angle)[:, None], np.sin(angle)[:, None]

    upper = np.array([False, True])[:, None]
    factors = Factors(note, lambda a, b: np.where(upper, b, a))
    unit = np.eye(SIDE).reshape(TILES, 2, SIDE)
    outs = real_forward([unit[t] for t in range(TILES)], SIDE, factors)
    outs = [np.stack([o[0] + o[1], o[0] - o[1]]) for o in outs]
    basis = np.concatenate(outs, 0)
    for size, t in wanted:
        angle = 2.0 * math.pi * (2 * t + np.repeat(np.arange(2), SIDE)) / size
        place[(size, t)] = len(rows)
        rows.append(np.cos(angle))
        rows.append(np.sin(angle))
    return np.stack(rows), place, basis


FACTOR_ROWS, FACTOR_PLACE, BASIS = factor_rows()


def tables():
    laplace = 2.0 * np.eye(SIDE) - np.roll(np.eye(SIDE), 1, 0) - np.roll(np.eye(SIDE), -1, 0)
    norms = np.sum(BASIS**2, 1)
    eigen_y = np.sum((BASIS @ laplace) * BASIS, 1) / norms
    points = np.arange(SIDE)
    eigen_z = 2.0 - 2.0 * np.cos(2.0 * math.pi * points / SIDE)
    mu = 1.0 / SIDE**2 + eigen_y[:, None] + eigen_z[None, :]
    ratio = 1.0 / (1.0 + mu / 2.0 + np.sqrt(mu + mu**2 / 4.0))
    scale = 1.0 / SIDE / (1.0 / ratio - ratio) / norms[:, None] / SIDE
    ratio = ratio.reshape(TILES, LANES)
    scale = scale.reshape(TILES, LANES)
    angle = 2.0 * math.pi * (points[:, None] * points[None, :] % SIDE) / SIDE
    along_z = np.cos(angle) + np.sin(angle)
    matrix = np.kron(np.array([[1.0, 1.0], [1.0, -1.0]]), along_z)
    high = matrix.astype(np.float32).astype(ml_dtypes.bfloat16)
    low = (matrix - high.astype(np.float64)).astype(ml_dtypes.bfloat16)
    row = np.concatenate([high, low], 1)
    weights = np.concatenate([row, row], 0)
    step = np.arange(8)[None, :, None]
    scans = []
    for hop in (1, 2, 4):
        scans.append(np.where(step >= hop, (ratio**hop)[:, None, :], 0.0))
    for hop in (1, 2, 4):
        scans.append(np.where(step < 8 - hop, (ratio**hop)[:, None, :], 0.0))
    spread = [ratio[:, None, :] ** (step + 1), ratio[:, None, :] ** (8 - step)]
    plain = [scale, ratio**8, ratio**32, 1.0 / (1.0 - ratio**64)]
    return (
        np.repeat(FACTOR_ROWS[:, None, :], 8, 1).astype(np.float32),
        weights,
        np.stack(scans).astype(np.float32),
        np.stack(spread).astype(np.float32),
        np.stack(plain).astype(np.float32),
    )


FACTOR_TABLE, WEIGHTS, SCAN_TABLE, SPREAD_TABLE, PLAIN_TABLE = tables()


def kernel_factors(factor_ref):
    lane = lax.broadcasted_iota(jnp.int32, (8, LANES), 1)
    upper = lane >= SIDE

    def fetch(size, t):
        at = FACTOR_PLACE[(size, t)]
        return factor_ref[at], factor_ref[at + 1]

    return Factors(fetch, lambda a, b: jnp.where(upper, b, a))


def lanes_of(t):
    return pl.ds(t * LANES, LANES)


def transform_rows(values, weights):
    high = values.astype(jnp.bfloat16)
    low = (values - high.astype(jnp.float32)).astype(jnp.bfloat16)
    both = jnp.concatenate([high, low], 1)
    out = jnp.dot(both, weights, preferred_element_type=jnp.float32)
    return out[:, :LANES] + out[:, LANES:]


def fill_window(sources, window, sems):
    copies = [
        pltpu.make_async_copy(ref, window.at[pl.ds(2 * n, 2)], sems.at[n])
        for n, ref in enumerate(sources)
    ]
    for copy in copies:
        copy.start()
    return copies


def pair_rows(ints_ref, slot):
    first = ints_ref[2 * slot]
    partner = ints_ref[2 * slot + 1]
    alive = slot < ints_ref[8]
    hop = lax.rem(partner // 2 - ints_ref[9] + ints_ref[10], ints_ref[10])
    second = 2 * hop + lax.rem(partner, 2)
    return jnp.where(alive, first, 0), jnp.where(alive, second, 0), alive


def forward_kernel(
    rows,
    ints_ref, prev_ref, own_ref, next_ref, factor_ref, weight_ref, scan_ref, plain_ref,
    local_ref, edge_ref,
    window, stage, spectrum, sems,
):
    copies = fill_window((prev_ref, own_ref, next_ref), window, sems)
    for copy in copies:
        copy.wait()
    factors = kernel_factors(factor_ref)
    octets = rows // 8

    def visit(slot, carry):
        first, second, alive = pair_rows(ints_ref, slot)
        weight = jnp.where(alive, 1.0, 0.0).astype(jnp.float32)
        for o in range(octets):
            span = pl.ds(8 * o, 8)
            values = []
            for t in range(TILES):
                left = window[first, span, lanes_of(t)]
                right = window[second, span, lanes_of(t)]
                values.append(left * right * weight)
            values = real_forward(values, SIDE, factors)
            for t in range(TILES):
                stage[o, t] = values[t]
        for o in range(octets):
            flat = stage[o].reshape(TILES * 8, LANES)
            spectrum[...] = transform_rows(flat, weight_ref[...]).reshape(TILES, 8, LANES)
            for t in range(TILES):
                value = spectrum[t] * plain_ref[0, pl.ds(t, 1), :]
                ahead = value
                behind = value
                for n, hop in enumerate((1, 2, 4)):
                    ahead = ahead + scan_ref[n, t] * pltpu.roll(ahead, hop, 0)
                    behind = behind + scan_ref[3 + n, t] * pltpu.roll(behind, 8 - hop, 0)
                local_ref[slot, o, t] = ahead + behind - value
                edge_ref[slot, o, 0, pl.ds(t, 1), :] = ahead[7:8]
                edge_ref[slot, o, 1, pl.ds(t, 1), :] = behind[0:1]
        return carry

    lax.fori_loop(0, 4, visit, 0)


def back_kernel(
    rows, begin, total,
    ints_ref, prev_ref, own_ref, next_ref, local_ref, edge_ref, other_ref,
    factor_ref, weight_ref, spread_ref, plain_ref,
    to_prev_ref, to_own_ref, to_next_ref,
    window, result, stage, fields, inflow, sems, out_sems,
):
    copies = fill_window((prev_ref, own_ref, next_ref), window, sems)
    result[...] = jnp.zeros_like(result)
    for copy in copies:
        copy.wait()
    factors = kernel_factors(factor_ref)
    octets = rows // 8

    def visit(slot, carry):
        first, second, alive = pair_rows(ints_ref, slot)
        weight = jnp.where(alive, 1.0, 0.0).astype(jnp.float32)
        step8, step32, closing = plain_ref[1], plain_ref[2], plain_ref[3]
        ahead_edges = [edge_ref[slot, o, 0] for o in range(total)]
        behind_edges = [edge_ref[slot, o, 1] for o in range(total)]

        def merged(edges):
            value = edges[0]
            for edge in edges[1:]:
                value = value * step8 + edge
            return value

        state = (other_ref[slot, 0] + step32 * merged(ahead_edges)) * closing
        for o in range(begin + octets):
            if o >= begin:
                inflow[o - begin, 0] = state
            state = state * step8 + ahead_edges[o]
        state = (other_ref[slot, 1] + step32 * merged(behind_edges[::-1])) * closing
        for o in range(total - 1, begin - 1, -1):
            if o < begin + octets:
                inflow[o - begin, 1] = state
            state = state * step8 + behind_edges[o]
        for o in range(octets):
            for t in range(TILES):
                value = local_ref[slot, o, t]
                value = value + spread_ref[0, t] * inflow[o, 0, pl.ds(t, 1), :]
                stage[t] = value + spread_ref[1, t] * inflow[o, 1, pl.ds(t, 1), :]
            flat = stage[...].reshape(TILES * 8, LANES)
            fields[...] = transform_rows(flat, weight_ref[...]).reshape(TILES, 8, LANES)
            values = real_back([fields[t] for t in range(TILES)], SIDE, factors)
            span = pl.ds(8 * o, 8)
            for t in range(TILES):
                value = values[t] * weight
                left = window[first, span, lanes_of(t)]
                right = window[second, span, lanes_of(t)]
                result[first, span, lanes_of(t)] += value * right
                result[second, span, lanes_of(t)] += value * left
        return carry

    lax.fori_loop(0, 4, visit, 0)
    copies = [
        pltpu.make_async_copy(result.at[pl.ds(2 * n, 2)], ref, out_sems.at[n])
        for n, ref in enumerate((to_prev_ref, to_own_ref, to_next_ref))
    ]
    for copy in copies:
        copy.start()
    for copy in copies:
        copy.wait()


ANY = pl.BlockSpec(memory_space=pl.ANY)
VMEM = pl.BlockSpec(memory_space=pltpu.VMEM)
SMEM = pl.BlockSpec(memory_space=pltpu.SMEM)
LIMIT = pltpu.CompilerParams(vmem_limit_bytes=48 * 1024 * 1024)


def forward(ints, prev, own, following):
    rows = own.shape[1]
    octets = rows // 8
    return pl.pallas_call(
        functools.partial(forward_kernel, rows),
        out_shape=(
            jax.ShapeDtypeStruct((4, octets, TILES, 8, LANES), jnp.float32),
            jax.ShapeDtypeStruct((4, octets, 2, TILES, LANES), jnp.float32),
        ),
        in_specs=[SMEM, ANY, ANY, ANY, VMEM, VMEM, VMEM, VMEM],
        out_specs=(VMEM, VMEM),
        scratch_shapes=[
            pltpu.VMEM((6, rows, SIDE * SIDE), jnp.float32),
            pltpu.VMEM((octets, TILES, 8, LANES), jnp.float32),
            pltpu.VMEM((TILES, 8, LANES), jnp.float32),
            pltpu.SemaphoreType.DMA((3,)),
        ],
        compiler_params=LIMIT,
        name="forward",
    )(ints, prev, own, following, FACTOR_TABLE, WEIGHTS, SCAN_TABLE, PLAIN_TABLE)


def back(ints, prev, own, following, local, edges, other, begin):
    rows = own.shape[1]
    octets = rows // 8
    block = jax.ShapeDtypeStruct(own.shape, jnp.float32)
    return pl.pallas_call(
        functools.partial(back_kernel, rows, begin, edges.shape[1]),
        out_shape=(block, block, block),
        in_specs=[SMEM, ANY, ANY, ANY, VMEM, VMEM, VMEM, VMEM, VMEM, VMEM, VMEM],
        out_specs=(ANY, ANY, ANY),
        scratch_shapes=[
            pltpu.VMEM((6, rows, SIDE * SIDE), jnp.float32),
            pltpu.VMEM((6, rows, SIDE * SIDE), jnp.float32),
            pltpu.VMEM((TILES, 8, LANES), jnp.float32),
            pltpu.VMEM((TILES, 8, LANES), jnp.float32),
            pltpu.VMEM((octets, 2, TILES, LANES), jnp.float32),
            pltpu.SemaphoreType.DMA((3,)),
            pltpu.SemaphoreType.DMA((3,)),
        ],
        compiler_params=LIMIT,
        name="back",
    )(
        ints, prev, own, following, local, edges, other,
        FACTOR_TABLE, WEIGHTS, SPREAD_TABLE, PLAIN_TABLE,
    )


def shifted(value, axis, steps):
    count = lax.axis_size(axis)
    pairs = [(source, (source + steps) % count) for source in range(count)]
    return lax.ppermute(value, axis, pairs)


def on_device(orbitals, pair_list, pair_count):
    band_count = lax.axis_size("band")
    group = lax.rem(lax.axis_index("band") + band_count - 1, band_count)
    rows = orbitals.shape[1] // CHUNKS
    own = [lax.slice_in_dim(orbitals, c * rows, (c + 1) * rows, axis=1) for c in range(CHUNKS)]
    ints = jnp.concatenate([pair_list.reshape(-1), pair_count])
    ints = shifted(ints, "band", 1)
    ints = jnp.concatenate([ints, jnp.stack([group, jnp.int32(band_count)]).astype(jnp.int32)])
    prev = [shifted(part, "band", 1) for part in own]
    following = [shifted(part, "band", -1) for part in own]
    local, edges = [], []
    for c in range(CHUNKS):
        field, edge = forward(ints, prev[c], own[c], following[c])
        local.append(field)
        edges.append(edge)
    edges = jnp.concatenate(edges, 1) if CHUNKS > 1 else edges[0]
    step8 = jnp.asarray(PLAIN_TABLE[1])
    ahead, behind = edges[:, 0, 0], edges[:, -1, 1]
    for o in range(1, edges.shape[1]):
        ahead = ahead * step8 + edges[:, o, 0]
        behind = behind * step8 + edges[:, -1 - o, 1]
    other = shifted(jnp.stack([ahead, behind], 1), "grid", 1)
    parts = []
    for c in range(CHUNKS):
        to_prev, to_own, to_next = back(
            ints, prev[c], own[c], following[c], local[c], edges, other, c * rows // 8
        )
        parts.append(to_own + shifted(to_prev, "band", -1) + shifted(to_next, "band", 1))
    return jnp.concatenate(parts, 1) if CHUNKS > 1 else parts[0]


def solution(mesh):
    in_specs = (P("band", "grid", None), P("band", None, None), P("band"))
    out_specs = P("band", "grid", None)
    return jax.shard_map(
        on_device, mesh=mesh, in_specs=in_specs, out_specs=out_specs, check_vma=False
    )
```

```python
import functools
import math

import jax
import jax.numpy as jnp
import ml_dtypes
import numpy as np
from jax import lax
from jax.experimental import pallas as pl
from jax.experimental.pallas import tpu as pltpu
from jax.sharding import PartitionSpec as P

SIDE = 64
TILES = SIDE // 2
LANES = 2 * SIDE
BACK_CHUNKS = 1
GROUPS = TILES // 8
FACTORS = 36


class Factors:
    def __init__(self, fetch, swap):
        self.fetch = fetch
        self.swap = swap


def turn(re, im, c, s):
    return re * c + im * s, im * c - re * s


def turn_back(re, im, c, s):
    return re * c - im * s, im * c + re * s


def complex_forward(re, im, size, factors):
    tiles = size // 2
    if tiles == 1:
        return [re[0], im[0]]
    half = tiles // 2
    even_re = [re[t] + re[t + half] for t in range(half)]
    even_im = [im[t] + im[t + half] for t in range(half)]
    odd_re, odd_im = [], []
    for t in range(half):
        a, b = re[t] - re[t + half], im[t] - im[t + half]
        if size == 4:
            a, b = factors.swap(a, b), factors.swap(b, -a)
        else:
            a, b = turn(a, b, *factors.fetch(size, t))
        odd_re.append(a)
        odd_im.append(b)
    return complex_forward(even_re, even_im, size // 2, factors) + complex_forward(
        odd_re, odd_im, size // 2, factors
    )


def complex_back(parts, size, factors):
    tiles = size // 2
    if tiles == 1:
        return [parts[0]], [parts[1]]
    half = tiles // 2
    even_re, even_im = complex_back(parts[:tiles], size // 2, factors)
    odd_re, odd_im = complex_back(parts[tiles:], size // 2, factors)
    low_re, low_im, high_re, high_im = [], [], [], []
    for t in range(half):
        a, b = odd_re[t], odd_im[t]
        if size == 4:
            a, b = factors.swap(a, -b), factors.swap(b, a)
        else:
            a, b = turn_back(a, b, *factors.fetch(size, t))
        low_re.append(even_re[t] + a)
        low_im.append(even_im[t] + b)
        high_re.append(even_re[t] - a)
        high_im.append(even_im[t] - b)
    return low_re + high_re, low_im + high_im


def real_forward(values, size, factors):
    tiles = size // 2
    if tiles == 1:
        return list(values)
    half = tiles // 2
    sums = [values[t] + values[t + half] for t in range(half)]
    rests = [values[t] - values[t + half] for t in range(half)]
    if size == 4:
        odd = rests
    else:
        quarter = half // 2
        re, im = [], []
        for t in range(quarter):
            a, b = turn(rests[t], -rests[t + quarter], *factors.fetch(size, t))
            re.append(a)
            im.append(b)
        odd = complex_forward(re, im, size // 4, factors)
    return real_forward(sums, size // 2, factors) + odd


def real_back(parts, size, factors):
    tiles = size // 2
    if tiles == 1:
        return list(parts)
    half = tiles // 2
    sums = real_back(parts[:half], size // 2, factors)
    if size == 4:
        rests = parts[half:]
    else:
        re, im = complex_back(parts[half:], size // 4, factors)
        quarter = half // 2
        low, high = [], []
        for t in range(quarter):
            a, b = turn_back(re[t], im[t], *factors.fetch(size, t))
            low.append(a)
            high.append(-b)
        rests = low + high
    return [sums[t] + rests[t] for t in range(half)] + [sums[t] - rests[t] for t in range(half)]


def factor_rows():
    rows, place, wanted = [], {}, []

    def note(size, t):
        if (size, t) not in wanted:
            wanted.append((size, t))
        angle = 2.0 * math.pi * (2 * t + np.arange(2)) / size
        return np.cos(angle)[:, None], np.sin(angle)[:, None]

    upper = np.array([False, True])[:, None]
    factors = Factors(note, lambda a, b: np.where(upper, b, a))
    unit = np.eye(SIDE).reshape(TILES, 2, SIDE)
    outs = real_forward([unit[t] for t in range(TILES)], SIDE, factors)
    outs = [np.stack([o[0] + o[1], o[0] - o[1]]) for o in outs]
    basis = np.concatenate(outs, 0)
    for size, t in wanted:
        angle = 2.0 * math.pi * (2 * t + np.repeat(np.arange(2), SIDE)) / size
        place[(size, t)] = len(rows)
        rows.append(np.cos(angle))
        rows.append(np.sin(angle))
    return np.stack(rows), place, basis


FACTOR_ROWS, FACTOR_PLACE, BASIS = factor_rows()


def tables():
    laplace = 2.0 * np.eye(SIDE) - np.roll(np.eye(SIDE), 1, 0) - np.roll(np.eye(SIDE), -1, 0)
    norms = np.sum(BASIS**2, 1)
    eigen_y = np.sum((BASIS @ laplace) * BASIS, 1) / norms
    points = np.arange(SIDE)
    eigen_z = 2.0 - 2.0 * np.cos(2.0 * math.pi * points / SIDE)
    mu = 1.0 / SIDE**2 + eigen_y[:, None] + eigen_z[None, :]
    ratio = 1.0 / (1.0 + mu / 2.0 + np.sqrt(mu + mu**2 / 4.0))
    scale = 1.0 / SIDE / (1.0 / ratio - ratio) / norms[:, None] / SIDE
    ratio = ratio.reshape(TILES, LANES)
    scale = scale.reshape(TILES, LANES)
    angle = 2.0 * math.pi * (points[:, None] * points[None, :] % SIDE) / SIDE
    along_z = np.cos(angle) + np.sin(angle)
    matrix = np.kron(np.array([[1.0, 1.0], [1.0, -1.0]]), along_z)
    high = matrix.astype(np.float32).astype(ml_dtypes.bfloat16)
    low = (matrix - high.astype(np.float64)).astype(ml_dtypes.bfloat16)
    row = np.concatenate([high, low], 1)
    weights = np.concatenate([row, row], 0)
    rows = SIDE // 2 // BACK_CHUNKS
    plain = np.stack([ratio, scale, ratio**rows, ratio**32, 1.0 / (1.0 - ratio**64)])
    factors = np.repeat(FACTOR_ROWS[:, None, :], 8, 1)
    table = np.concatenate([factors, plain.reshape(-1, 8, LANES)], 0)
    return weights, table.astype(np.float32)


WEIGHTS, TABLE = tables()
assert len(FACTOR_ROWS) == FACTORS


def kernel_factors(table_ref):
    lane = lax.broadcasted_iota(jnp.int32, (8, LANES), 1)
    upper = lane >= SIDE

    def fetch(size, t):
        at = FACTOR_PLACE[(size, t)]
        return table_ref[at], table_ref[at + 1]

    return Factors(fetch, lambda a, b: jnp.where(upper, b, a))


def plain(table_ref, kind, group):
    return table_ref[FACTORS + GROUPS * kind + group]


def lanes_of(t):
    return pl.ds(t * LANES, LANES)


def transform_rows(values, weights):
    high = values.astype(jnp.bfloat16)
    low = (values - high.astype(jnp.float32)).astype(jnp.bfloat16)
    both = jnp.concatenate([high, low], 1)
    out = jnp.dot(both, weights, preferred_element_type=jnp.float32)
    return out[:, :LANES] + out[:, LANES:]


def pair_rows(ints_ref, slot):
    groups = lax.axis_size("band")
    below = lax.axis_index("band") + groups - 1
    first = ints_ref[2 * slot]
    partner = ints_ref[2 * slot + 1]
    alive = slot < ints_ref[8]
    hop = lax.rem(partner // 2 - lax.rem(below, groups) + groups, groups)
    second = 2 * hop + lax.rem(partner, 2)
    return jnp.where(alive, first, 0), jnp.where(alive, second, 0), alive


def cross_at():
    return 4 * lax.rem(lax.axis_index("band"), 2)


def prepare_kernel(
    pairs_ref, count_ref, own_ref, weight_ref, table_ref,
    ints_ref, window, weights, table, sems,
):
    copies = [
        pltpu.make_async_copy(own_ref, window.at[pl.ds(2, 2)], sems.at[0]),
        pltpu.make_async_copy(weight_ref, weights, sems.at[1]),
        pltpu.make_async_copy(table_ref, table, sems.at[2]),
    ]
    for copy in copies:
        copy.start()
    for n in range(4):
        ints_ref[2 * n] = pairs_ref[0, n, 0]
        ints_ref[2 * n + 1] = pairs_ref[0, n, 1]
    ints_ref[8] = count_ref[0]
    for copy in copies:
        copy.wait()


def forward_kernel(
    ints_ref, mate_ref, cross_ref, window_ref, weights, table,
    local_ref, edge_ref, window,
    stage, sems,
):
    rows = window.shape[1]
    cross = cross_at()
    copies = [
        pltpu.make_async_copy(mate_ref, window.at[pl.ds(4 - cross, 2)], sems.at[0]),
        pltpu.make_async_copy(cross_ref, window.at[pl.ds(cross, 2)], sems.at[1]),
    ]
    for copy in copies:
        copy.start()
    for copy in copies:
        copy.wait()
    factors = kernel_factors(table)

    def along_y(slot):
        first, second, alive = pair_rows(ints_ref, slot)
        for o in range(rows // 8):
            values = []
            for t in range(TILES):
                left = window[first, pl.ds(8 * o, 8), lanes_of(t)]
                right = window[second, pl.ds(8 * o, 8), lanes_of(t)]
                values.append(left * right)
            values = real_forward(values, SIDE, factors)
            for t in range(TILES):
                stage[slot, pl.ds((o * TILES + t) * 8, 8)] = values[t]

    def along_zx(slot, g):
        alive = pair_rows(ints_ref, slot)[2]
        weight = jnp.where(alive, 1.0, 0.0).astype(jnp.float32)
        parts = [
            stage[slot, pl.ds(x // 8 * TILES * 8 + g * 64 + x % 8, 8, stride=8)]
            for x in range(rows)
        ]
        spectrum = transform_rows(jnp.concatenate(parts, 0), weights[...])
        ratio, scale = plain(table, 0, g), plain(table, 1, g) * weight
        values = [spectrum[8 * x : 8 * x + 8] * scale for x in range(rows)]
        ahead = values[0]
        sums = [ahead]
        for x in range(1, rows):
            ahead = ahead * ratio
            sums.append(ahead)
            ahead = ahead + values[x]
        behind = values[rows - 1]
        local_ref[slot, g, rows - 1] = sums[rows - 1] + behind
        for x in range(rows - 2, -1, -1):
            behind = behind * ratio + values[x]
            local_ref[slot, g, x] = (sums[x] + behind) if x else behind
        edge_ref[slot, 0, g] = ahead
        edge_ref[slot, 1, g] = behind

    along_y(0)
    for slot in range(4):
        if slot < 3:
            along_y(slot + 1)
        for g in range(GROUPS):
            along_zx(slot, g)


def back_kernel(
    rows, chunk,
    ints_ref, window, local_ref, edge_ref, other_ref, weights, table, *rest,
):
    if chunk:
        rest = rest[2:]
    cross_ref, mate_ref, own_ref, result, fields, out_sems = rest
    cross = cross_at()
    begin = chunk * rows
    result[...] = jnp.zeros_like(result)
    factors = kernel_factors(table)

    def along_xz(slot, g):
        ratio, step = plain(table, 0, g), plain(table, 2, g)
        whole, closing = plain(table, 3, g), plain(table, 4, g)
        ahead = (other_ref[slot, 0, g] + whole * edge_ref[slot, 0, g]) * closing
        for _ in range(chunk):
            ahead = ahead * step
        behind = (other_ref[slot, 1, g] + whole * edge_ref[slot, 1, g]) * closing
        for _ in range(BACK_CHUNKS - 1 - chunk):
            behind = behind * step
        behinds = []
        for x in range(rows):
            behind = behind * ratio
            behinds.append(behind)
        parts = []
        for x in range(rows):
            ahead = ahead * ratio
            parts.append(local_ref[slot, g, begin + x] + (ahead + behinds[rows - 1 - x]))
        values = transform_rows(jnp.concatenate(parts, 0), weights[...])
        for x in range(rows):
            fields[slot, pl.ds(x * TILES + 8 * g, 8)] = values[8 * x : 8 * x + 8]

    def along_y(slot):
        first, second, alive = pair_rows(ints_ref, slot)
        for o in range(rows // 8):
            values = [
                fields[slot, pl.ds(8 * o * TILES + t, 8, stride=TILES)] for t in range(TILES)
            ]
            values = real_back(values, SIDE, factors)
            here = pl.ds(8 * o, 8)
            there = pl.ds(begin + 8 * o, 8)
            for begin_t in range(0, TILES, 8):
                new = []
                for t in range(begin_t, begin_t + 8):
                    left = window[first, there, lanes_of(t)]
                    right = window[second, there, lanes_of(t)]
                    new.append((
                        result[first, here, lanes_of(t)] + values[t] * right,
                        result[second, here, lanes_of(t)] + values[t] * left,
                    ))
                for t in range(begin_t, begin_t + 8):
                    result[first, here, lanes_of(t)] = new[t - begin_t][0]
                for t in range(begin_t, begin_t + 8):
                    result[second, here, lanes_of(t)] = new[t - begin_t][1]

    for slot in range(5):
        if slot < 4:
            for g in range(GROUPS):
                along_xz(slot, g)
        if slot:
            along_y(slot - 1)
    span = pl.ds(begin, rows)
    copies = [
        pltpu.make_async_copy(result.at[pl.ds(cross, 2)], cross_ref, out_sems.at[0]),
        pltpu.make_async_copy(result.at[pl.ds(4 - cross, 2)], mate_ref.at[:, span], out_sems.at[1]),
        pltpu.make_async_copy(result.at[pl.ds(2, 2)], own_ref.at[:, span], out_sems.at[2]),
    ]
    for copy in copies:
        copy.start()
    for copy in copies:
        copy.wait()


ANY = pl.BlockSpec(memory_space=pl.ANY)
HBM = pl.BlockSpec(memory_space=pltpu.HBM)
VMEM = pl.BlockSpec(memory_space=pltpu.VMEM)
SMEM = pl.BlockSpec(memory_space=pltpu.SMEM)
LIMIT = pltpu.CompilerParams(vmem_limit_bytes=20 * 1024 * 1024)
COST = pl.CostEstimate(flops=0, bytes_accessed=12_000_000, transcendentals=0)


def prepare(pair_list, pair_count, own):
    rows = own.shape[1]
    return pl.pallas_call(
        prepare_kernel,
        out_shape=(
            jax.ShapeDtypeStruct((9,), jnp.int32),
            jax.ShapeDtypeStruct((6, rows, SIDE * SIDE), jnp.float32),
            jax.ShapeDtypeStruct(WEIGHTS.shape, jnp.bfloat16),
            jax.ShapeDtypeStruct(TABLE.shape, jnp.float32),
        ),
        in_specs=[SMEM, SMEM, HBM, HBM, HBM],
        out_specs=(SMEM, VMEM, VMEM, VMEM),
        scratch_shapes=[pltpu.SemaphoreType.DMA((3,))],
        compiler_params=LIMIT,
        name="prepare",
    )(pair_list, pair_count, own, WEIGHTS, TABLE)


def forward(ints, mate, cross, window, weights, table):
    rows = window.shape[1]
    return pl.pallas_call(
        forward_kernel,
        out_shape=(
            jax.ShapeDtypeStruct((4, GROUPS, rows, 8, LANES), jnp.float32),
            jax.ShapeDtypeStruct((4, 2, GROUPS, 8, LANES), jnp.float32),
            jax.ShapeDtypeStruct((6, rows, SIDE * SIDE), jnp.float32),
        ),
        in_specs=[SMEM, ANY, ANY, VMEM, VMEM, VMEM],
        out_specs=(VMEM, VMEM, VMEM),
        input_output_aliases={3: 2},
        scratch_shapes=[
            pltpu.VMEM((4, rows * TILES, LANES), jnp.float32),
            pltpu.SemaphoreType.DMA((2,)),
        ],
        compiler_params=LIMIT,
        cost_estimate=COST,
        name="forward",
    )(ints, mate, cross, window, weights, table)


def back(ints, window, local, edges, other, weights, table, chunk, carried):
    rows = window.shape[1] // BACK_CHUNKS
    part = jax.ShapeDtypeStruct((2, rows, SIDE * SIDE), jnp.float32)
    block = jax.ShapeDtypeStruct((2, rows * BACK_CHUNKS, SIDE * SIDE), jnp.float32)
    return pl.pallas_call(
        functools.partial(back_kernel, rows, chunk),
        out_shape=(part, block, block),
        in_specs=[SMEM] + [VMEM] * 6 + [ANY] * len(carried),
        out_specs=(ANY, ANY, ANY),
        input_output_aliases={7: 1, 8: 2} if carried else {},
        scratch_shapes=[
            pltpu.VMEM((6, rows, SIDE * SIDE), jnp.float32),
            pltpu.VMEM((4, rows * TILES, LANES), jnp.float32),
            pltpu.SemaphoreType.DMA((3,)),
        ],
        compiler_params=LIMIT,
        cost_estimate=COST,
        name="back",
    )(ints, window, local, edges, other, weights, table, *carried)


def moved(value, axis, target):
    count = lax.axis_size(axis)
    return lax.ppermute(value, axis, [(n, target(n) % count) for n in range(count)])


def to_mate(value):
    return moved(value, "band", lambda n: n ^ 1)


def to_cross(value):
    return moved(value, "band", lambda n: n + 1 if n % 2 else n - 1)


def on_device(orbitals, pair_list, pair_count):
    cross = to_cross(orbitals)
    ints, window, weights, table = prepare(pair_list, pair_count, orbitals)
    held, ints = lax.optimization_barrier((orbitals, ints))
    ints = moved(ints, "band", lambda n: n + 1)
    mate = to_mate(held)
    local, edges, window = forward(ints, mate, cross, window, weights, table)
    other = moved(edges, "grid", lambda n: n + 1)
    returned, carried = [], ()
    for chunk in range(BACK_CHUNKS):
        part, *carried = back(ints, window, local, edges, other, weights, table, chunk, carried)
        returned.append(to_cross(part))
    mate, own = carried
    return (own + returned[0]) + to_mate(mate)


def solution(mesh):
    in_specs = (P("band", "grid", None), P("band", None, None), P("band"))
    out_specs = P("band", "grid", None)
    return jax.shard_map(
        on_device, mesh=mesh, in_specs=in_specs, out_specs=out_specs, check_vma=False
    )
```

```python
import functools
import math

import jax
import jax.numpy as jnp
import ml_dtypes
import numpy as np
from jax import lax
from jax.experimental import pallas as pl
from jax.experimental.pallas import tpu as pltpu
from jax.sharding import PartitionSpec as P

SIDE = 64
TILES = SIDE // 2
LANES = 2 * SIDE
GROUPS = TILES // 8
FACTORS = 36


class Factors:
    def __init__(self, fetch, swap):
        self.fetch = fetch
        self.swap = swap


def turn(re, im, c, s):
    return re * c + im * s, im * c - re * s


def turn_back(re, im, c, s):
    return re * c - im * s, im * c + re * s


def complex_forward(re, im, size, factors):
    tiles = size // 2
    if tiles == 1:
        return [re[0], im[0]]
    half = tiles // 2
    even_re = [re[t] + re[t + half] for t in range(half)]
    even_im = [im[t] + im[t + half] for t in range(half)]
    odd_re, odd_im = [], []
    for t in range(half):
        a, b = re[t] - re[t + half], im[t] - im[t + half]
        if size == 4:
            a, b = factors.swap(a, b), factors.swap(b, -a)
        else:
            a, b = turn(a, b, *factors.fetch(size, t))
        odd_re.append(a)
        odd_im.append(b)
    return complex_forward(even_re, even_im, size // 2, factors) + complex_forward(
        odd_re, odd_im, size // 2, factors
    )


def complex_back(parts, size, factors):
    tiles = size // 2
    if tiles == 1:
        return [parts[0]], [parts[1]]
    half = tiles // 2
    even_re, even_im = complex_back(parts[:tiles], size // 2, factors)
    odd_re, odd_im = complex_back(parts[tiles:], size // 2, factors)
    low_re, low_im, high_re, high_im = [], [], [], []
    for t in range(half):
        a, b = odd_re[t], odd_im[t]
        if size == 4:
            a, b = factors.swap(a, -b), factors.swap(b, a)
        else:
            a, b = turn_back(a, b, *factors.fetch(size, t))
        low_re.append(even_re[t] + a)
        low_im.append(even_im[t] + b)
        high_re.append(even_re[t] - a)
        high_im.append(even_im[t] - b)
    return low_re + high_re, low_im + high_im


def real_forward(values, size, factors):
    tiles = size // 2
    if tiles == 1:
        return list(values)
    half = tiles // 2
    sums = [values[t] + values[t + half] for t in range(half)]
    rests = [values[t] - values[t + half] for t in range(half)]
    if size == 4:
        odd = rests
    else:
        quarter = half // 2
        re, im = [], []
        for t in range(quarter):
            a, b = turn(rests[t], -rests[t + quarter], *factors.fetch(size, t))
            re.append(a)
            im.append(b)
        odd = complex_forward(re, im, size // 4, factors)
    return real_forward(sums, size // 2, factors) + odd


def real_back(parts, size, factors):
    tiles = size // 2
    if tiles == 1:
        return list(parts)
    half = tiles // 2
    sums = real_back(parts[:half], size // 2, factors)
    if size == 4:
        rests = parts[half:]
    else:
        re, im = complex_back(parts[half:], size // 4, factors)
        quarter = half // 2
        low, high = [], []
        for t in range(quarter):
            a, b = turn_back(re[t], im[t], *factors.fetch(size, t))
            low.append(a)
            high.append(-b)
        rests = low + high
    return [sums[t] + rests[t] for t in range(half)] + [sums[t] - rests[t] for t in range(half)]


def factor_rows():
    rows, place, wanted = [], {}, []

    def note(size, t):
        if (size, t) not in wanted:
            wanted.append((size, t))
        angle = 2.0 * math.pi * (2 * t + np.arange(2)) / size
        return np.cos(angle)[:, None], np.sin(angle)[:, None]

    upper = np.array([False, True])[:, None]
    factors = Factors(note, lambda a, b: np.where(upper, b, a))
    unit = np.eye(SIDE).reshape(TILES, 2, SIDE)
    outs = real_forward([unit[t] for t in range(TILES)], SIDE, factors)
    outs = [np.stack([o[0] + o[1], o[0] - o[1]]) for o in outs]
    basis = np.concatenate(outs, 0)
    for size, t in wanted:
        angle = 2.0 * math.pi * (2 * t + np.repeat(np.arange(2), SIDE)) / size
        place[(size, t)] = len(rows)
        rows.append(np.cos(angle))
        rows.append(np.sin(angle))
    return np.stack(rows), place, basis


FACTOR_ROWS, FACTOR_PLACE, BASIS = factor_rows()


def tables():
    laplace = 2.0 * np.eye(SIDE) - np.roll(np.eye(SIDE), 1, 0) - np.roll(np.eye(SIDE), -1, 0)
    norms = np.sum(BASIS**2, 1)
    eigen_y = np.sum((BASIS @ laplace) * BASIS, 1) / norms
    points = np.arange(SIDE)
    eigen_z = 2.0 - 2.0 * np.cos(2.0 * math.pi * points / SIDE)
    mu = 1.0 / SIDE**2 + eigen_y[:, None] + eigen_z[None, :]
    ratio = 1.0 / (1.0 + mu / 2.0 + np.sqrt(mu + mu**2 / 4.0))
    scale = 1.0 / SIDE / (1.0 / ratio - ratio) / norms[:, None] / SIDE
    ratio = ratio.reshape(TILES, LANES)
    scale = scale.reshape(TILES, LANES)
    angle = 2.0 * math.pi * (points[:, None] * points[None, :] % SIDE) / SIDE
    along_z = np.cos(angle) + np.sin(angle)
    matrix = np.kron(np.array([[1.0, 1.0], [1.0, -1.0]]), along_z)
    high = matrix.astype(np.float32).astype(ml_dtypes.bfloat16)
    low = (matrix - high.astype(np.float64)).astype(ml_dtypes.bfloat16)
    row = np.concatenate([high, low], 1)
    weights = np.concatenate([row, row], 0)
    plain = np.stack([ratio, scale, ratio**32, 1.0 / (1.0 - ratio**64)])
    factors = np.repeat(FACTOR_ROWS[:, None, :], 8, 1)
    table = np.concatenate([factors, plain.reshape(-1, 8, LANES)], 0)
    return weights, table.astype(np.float32)


WEIGHTS, TABLE = tables()
assert len(FACTOR_ROWS) == FACTORS


def kernel_factors(table_ref):
    lane = lax.broadcasted_iota(jnp.int32, (8, LANES), 1)
    upper = lane >= SIDE

    def fetch(size, t):
        at = FACTOR_PLACE[(size, t)]
        return table_ref[at], table_ref[at + 1]

    return Factors(fetch, lambda a, b: jnp.where(upper, b, a))


def plain(table_ref, kind, group):
    return table_ref[FACTORS + GROUPS * kind + group]


def lanes_of(t):
    return pl.ds(t * LANES, LANES)


def transform_rows(values, weights):
    high = values.astype(jnp.bfloat16)
    low = (values - high.astype(jnp.float32)).astype(jnp.bfloat16)
    both = jnp.concatenate([high, low], 1)
    out = jnp.dot(both, weights, preferred_element_type=jnp.float32)
    return out[:, :LANES] + out[:, LANES:]


def pair_rows(ints_ref, slot):
    groups = lax.axis_size("band")
    below = lax.axis_index("band") + groups - 1
    first = ints_ref[2 * slot]
    partner = ints_ref[2 * slot + 1]
    alive = slot < ints_ref[8]
    hop = lax.rem(partner // 2 - lax.rem(below, groups) + groups, groups)
    second = 2 * hop + lax.rem(partner, 2)
    return jnp.where(alive, first, 0), jnp.where(alive, second, 0), alive


def cross_at():
    return 4 * lax.rem(lax.axis_index("band"), 2)


def pack_kernel(pairs_ref, count_ref, ints_ref):
    for n in range(4):
        ints_ref[2 * n] = pairs_ref[0, n, 0]
        ints_ref[2 * n + 1] = pairs_ref[0, n, 1]
    ints_ref[8] = count_ref[0]


def prepare_kernel(
    own_ref, weight_ref, table_ref,
    window, result, weights, table, sems,
):
    copies = [
        pltpu.make_async_copy(own_ref, window.at[pl.ds(2, 2)], sems.at[0]),
        pltpu.make_async_copy(weight_ref, weights, sems.at[1]),
        pltpu.make_async_copy(table_ref, table, sems.at[2]),
    ]
    for copy in copies:
        copy.start()
    result[...] = jnp.zeros_like(result)
    for copy in copies:
        copy.wait()


def forward_kernel(
    ints_ref, cross_ref, mate_ref, window_ref, weights, table,
    local_ref, edge_ref, window,
    stage, sems,
):
    rows = window.shape[1]
    cross = cross_at()
    copies = []
    for o in range(rows // 8):
        span = pl.ds(8 * o, 8)
        copies.append([
            pltpu.make_async_copy(ref.at[:, span], window.at[pl.ds(at, 2), span], sems.at[n, o])
            for n, (ref, at) in enumerate(((mate_ref, 4 - cross), (cross_ref, cross)))
        ])
        for copy in copies[o]:
            copy.start()
    factors = kernel_factors(table)

    def along_y(slot):
        first, second, alive = pair_rows(ints_ref, slot)
        for o in range(rows // 8):
            if slot == 0:
                for copy in copies[o]:
                    copy.wait()
            values = []
            for t in range(TILES):
                left = window[first, pl.ds(8 * o, 8), lanes_of(t)]
                right = window[second, pl.ds(8 * o, 8), lanes_of(t)]
                values.append(left * right)
            values = real_forward(values, SIDE, factors)
            for t in range(TILES):
                stage[slot, pl.ds((o * TILES + t) * 8, 8)] = values[t]

    def along_zx(slot, g):
        alive = pair_rows(ints_ref, slot)[2]
        weight = jnp.where(alive, 1.0, 0.0).astype(jnp.float32)
        parts = [
            stage[slot, pl.ds(x // 8 * TILES * 8 + g * 64 + x % 8, 8, stride=8)]
            for x in range(rows)
        ]
        spectrum = transform_rows(jnp.concatenate(parts, 0), weights[...])
        ratio, scale = plain(table, 0, g), plain(table, 1, g) * weight
        values = [spectrum[8 * x : 8 * x + 8] * scale for x in range(rows)]
        ahead = values[0]
        sums = [ahead]
        for x in range(1, rows):
            ahead = ahead * ratio
            sums.append(ahead)
            ahead = ahead + values[x]
        behind = values[rows - 1]
        local_ref[slot, g, rows - 1] = sums[rows - 1] + behind
        for x in range(rows - 2, -1, -1):
            behind = behind * ratio + values[x]
            local_ref[slot, g, x] = (sums[x] + behind) if x else behind
        edge_ref[slot, 0, g] = ahead
        edge_ref[slot, 1, g] = behind

    along_y(0)
    for slot in range(4):
        if slot < 3:
            along_y(slot + 1)
        for g in range(GROUPS):
            along_zx(slot, g)


def back_kernel(
    ints_ref, window, local_ref, edge_ref, other_ref, weights, table, zero_ref,
    cross_ref, mate_ref, own_ref, result,
    fields, sems,
):
    rows = window.shape[1]
    cross = cross_at()
    factors = kernel_factors(table)

    def along_xz(slot, g):
        ratio, whole, closing = [plain(table, kind, g) for kind in (0, 2, 3)]
        ahead = (other_ref[slot, 0, g] + whole * edge_ref[slot, 0, g]) * closing
        behind = (other_ref[slot, 1, g] + whole * edge_ref[slot, 1, g]) * closing
        behinds = []
        for x in range(rows):
            behind = behind * ratio
            behinds.append(behind)
        parts = []
        for x in range(rows):
            ahead = ahead * ratio
            parts.append(local_ref[slot, g, x] + (ahead + behinds[rows - 1 - x]))
        values = transform_rows(jnp.concatenate(parts, 0), weights[...])
        for x in range(rows):
            fields[slot, pl.ds(x * TILES + 8 * g, 8)] = values[8 * x : 8 * x + 8]

    def along_y(slot):
        first, second, alive = pair_rows(ints_ref, slot)
        for o in range(rows // 8):
            values = [
                fields[slot, pl.ds(8 * o * TILES + t, 8, stride=TILES)] for t in range(TILES)
            ]
            values = real_back(values, SIDE, factors)
            span = pl.ds(8 * o, 8)
            for begin_t in range(0, TILES, 8):
                new = []
                for t in range(begin_t, begin_t + 8):
                    left = window[first, span, lanes_of(t)]
                    right = window[second, span, lanes_of(t)]
                    new.append((
                        result[first, span, lanes_of(t)] + values[t] * right,
                        result[second, span, lanes_of(t)] + values[t] * left,
                    ))
                for t in range(begin_t, begin_t + 8):
                    result[first, span, lanes_of(t)] = new[t - begin_t][0]
                for t in range(begin_t, begin_t + 8):
                    result[second, span, lanes_of(t)] = new[t - begin_t][1]
            if slot == 3:
                for n, (ref, at) in enumerate(
                    ((cross_ref, cross), (mate_ref, 4 - cross), (own_ref, 2))
                ):
                    copies.append(pltpu.make_async_copy(
                        result.at[pl.ds(at, 2), span], ref.at[:, span], sems.at[n, o]
                    ))
                    copies[-1].start()

    copies = []
    for slot in range(5):
        if slot < 4:
            for g in range(GROUPS):
                along_xz(slot, g)
        if slot:
            along_y(slot - 1)
    for copy in copies:
        copy.wait()


ANY = pl.BlockSpec(memory_space=pl.ANY)
HBM = pl.BlockSpec(memory_space=pltpu.HBM)
VMEM = pl.BlockSpec(memory_space=pltpu.VMEM)
SMEM = pl.BlockSpec(memory_space=pltpu.SMEM)
LIMIT = pltpu.CompilerParams(vmem_limit_bytes=20 * 1024 * 1024)
COST = pl.CostEstimate(flops=0, bytes_accessed=12_000_000, transcendentals=0)


def pack(pair_list, pair_count):
    return pl.pallas_call(
        pack_kernel,
        out_shape=jax.ShapeDtypeStruct((9,), jnp.int32),
        in_specs=[SMEM, SMEM],
        out_specs=SMEM,
        name="pack",
    )(pair_list, pair_count)


def prepare(own):
    shape = (6,) + own.shape[1:]
    return pl.pallas_call(
        prepare_kernel,
        out_shape=(
            jax.ShapeDtypeStruct(shape, jnp.float32),
            jax.ShapeDtypeStruct(shape, jnp.float32),
            jax.ShapeDtypeStruct(WEIGHTS.shape, jnp.bfloat16),
            jax.ShapeDtypeStruct(TABLE.shape, jnp.float32),
        ),
        in_specs=[HBM, HBM, HBM],
        out_specs=(VMEM, VMEM, VMEM, VMEM),
        scratch_shapes=[pltpu.SemaphoreType.DMA((3,))],
        compiler_params=LIMIT,
        cost_estimate=COST,
        name="prepare",
    )(own, WEIGHTS, TABLE)


def forward(ints, cross, mate, window, weights, table):
    rows = window.shape[1]
    return pl.pallas_call(
        forward_kernel,
        out_shape=(
            jax.ShapeDtypeStruct((4, GROUPS, rows, 8, LANES), jnp.float32),
            jax.ShapeDtypeStruct((4, 2, GROUPS, 8, LANES), jnp.float32),
            jax.ShapeDtypeStruct((6, rows, SIDE * SIDE), jnp.float32),
        ),
        in_specs=[SMEM, ANY, ANY, VMEM, VMEM, VMEM],
        out_specs=(VMEM, VMEM, VMEM),
        input_output_aliases={3: 2},
        scratch_shapes=[
            pltpu.VMEM((4, rows * TILES, LANES), jnp.float32),
            pltpu.SemaphoreType.DMA((2, rows // 8)),
        ],
        compiler_params=LIMIT,
        cost_estimate=COST,
        name="forward",
    )(ints, cross, mate, window, weights, table)


def back(ints, window, local, edges, other, weights, table, result):
    rows = window.shape[1]
    block = jax.ShapeDtypeStruct((2, rows, SIDE * SIDE), jnp.float32)
    return pl.pallas_call(
        back_kernel,
        out_shape=(block, block, block, jax.ShapeDtypeStruct(result.shape, jnp.float32)),
        in_specs=[SMEM] + [VMEM] * 7,
        out_specs=(ANY, ANY, ANY, VMEM),
        input_output_aliases={7: 3},
        scratch_shapes=[
            pltpu.VMEM((4, rows * TILES, LANES), jnp.float32),
            pltpu.SemaphoreType.DMA((3, rows // 8)),
        ],
        compiler_params=LIMIT,
        cost_estimate=COST,
        name="back",
    )(ints, window, local, edges, other, weights, table, result)


def moved(value, axis, target):
    count = lax.axis_size(axis)
    return lax.ppermute(value, axis, [(n, target(n) % count) for n in range(count)])


def to_mate(value):
    return moved(value, "band", lambda n: n ^ 1)


def to_cross(value):
    return moved(value, "band", lambda n: n + 1 if n % 2 else n - 1)


def to_next_other_slab(value):
    count = lax.axis_size("band")
    pairs = [(2 * n + g, 2 * ((n + 1) % count) + 1 - g) for n in range(count) for g in range(2)]
    return lax.ppermute(value, ("band", "grid"), pairs)


def on_device(orbitals, pair_list, pair_count):
    cross = to_cross(orbitals)
    mate = to_mate(orbitals)
    ints = to_next_other_slab(pack(pair_list, pair_count))
    window, result, weights, table = prepare(orbitals)
    local, edges, window = forward(ints, cross, mate, window, weights, table)
    other = moved(edges, "grid", lambda n: n + 1)
    cross, mate, own, _ = back(ints, window, local, edges, other, weights, table, result)
    return (own + to_cross(cross)) + to_mate(mate)


def solution(mesh):
    in_specs = (P("band", "grid", None), P("band", None, None), P("band"))
    out_specs = P("band", "grid", None)
    return jax.shard_map(
        on_device, mesh=mesh, in_specs=in_specs, out_specs=out_specs, check_vma=False
    )
```

```python
import functools
import math

import jax
import jax.numpy as jnp
import ml_dtypes
import numpy as np
from jax import lax
from jax.experimental import pallas as pl
from jax.experimental.pallas import tpu as pltpu
from jax.sharding import PartitionSpec as P

SIDE = 64
TILES = SIDE // 2
LANES = 2 * SIDE
GROUPS = TILES // 8
FACTORS = 36


class Factors:
    def __init__(self, fetch, swap):
        self.fetch = fetch
        self.swap = swap


def turn(re, im, c, s):
    return re * c + im * s, im * c - re * s


def turn_back(re, im, c, s):
    return re * c - im * s, im * c + re * s


def complex_forward(re, im, size, factors):
    tiles = size // 2
    if tiles == 1:
        return [re[0], im[0]]
    half = tiles // 2
    even_re = [re[t] + re[t + half] for t in range(half)]
    even_im = [im[t] + im[t + half] for t in range(half)]
    odd_re, odd_im = [], []
    for t in range(half):
        a, b = re[t] - re[t + half], im[t] - im[t + half]
        if size == 4:
            a, b = factors.swap(a, b), factors.swap(b, -a)
        else:
            a, b = turn(a, b, *factors.fetch(size, t))
        odd_re.append(a)
        odd_im.append(b)
    return complex_forward(even_re, even_im, size // 2, factors) + complex_forward(
        odd_re, odd_im, size // 2, factors
    )


def complex_back(parts, size, factors):
    tiles = size // 2
    if tiles == 1:
        return [parts[0]], [parts[1]]
    half = tiles // 2
    even_re, even_im = complex_back(parts[:tiles], size // 2, factors)
    odd_re, odd_im = complex_back(parts[tiles:], size // 2, factors)
    low_re, low_im, high_re, high_im = [], [], [], []
    for t in range(half):
        a, b = odd_re[t], odd_im[t]
        if size == 4:
            a, b = factors.swap(a, -b), factors.swap(b, a)
        else:
            a, b = turn_back(a, b, *factors.fetch(size, t))
        low_re.append(even_re[t] + a)
        low_im.append(even_im[t] + b)
        high_re.append(even_re[t] - a)
        high_im.append(even_im[t] - b)
    return low_re + high_re, low_im + high_im


def real_forward(values, size, factors):
    tiles = size // 2
    if tiles == 1:
        return list(values)
    half = tiles // 2
    sums = [values[t] + values[t + half] for t in range(half)]
    rests = [values[t] - values[t + half] for t in range(half)]
    if size == 4:
        odd = rests
    else:
        quarter = half // 2
        re, im = [], []
        for t in range(quarter):
            a, b = turn(rests[t], -rests[t + quarter], *factors.fetch(size, t))
            re.append(a)
            im.append(b)
        odd = complex_forward(re, im, size // 4, factors)
    return real_forward(sums, size // 2, factors) + odd


def real_back(parts, size, factors):
    tiles = size // 2
    if tiles == 1:
        return list(parts)
    half = tiles // 2
    sums = real_back(parts[:half], size // 2, factors)
    if size == 4:
        rests = parts[half:]
    else:
        re, im = complex_back(parts[half:], size // 4, factors)
        quarter = half // 2
        low, high = [], []
        for t in range(quarter):
            a, b = turn_back(re[t], im[t], *factors.fetch(size, t))
            low.append(a)
            high.append(-b)
        rests = low + high
    return [sums[t] + rests[t] for t in range(half)] + [sums[t] - rests[t] for t in range(half)]


def factor_rows():
    rows, place, wanted = [], {}, []

    def note(size, t):
        if (size, t) not in wanted:
            wanted.append((size, t))
        angle = 2.0 * math.pi * (2 * t + np.arange(2)) / size
        return np.cos(angle)[:, None], np.sin(angle)[:, None]

    upper = np.array([False, True])[:, None]
    factors = Factors(note, lambda a, b: np.where(upper, b, a))
    unit = np.eye(SIDE).reshape(TILES, 2, SIDE)
    outs = real_forward([unit[t] for t in range(TILES)], SIDE, factors)
    outs = [np.stack([o[0] + o[1], o[0] - o[1]]) for o in outs]
    basis = np.concatenate(outs, 0)
    for size, t in wanted:
        angle = 2.0 * math.pi * (2 * t + np.repeat(np.arange(2), SIDE)) / size
        place[(size, t)] = len(rows)
        rows.append(np.cos(angle))
        rows.append(np.sin(angle))
    return np.stack(rows), place, basis


FACTOR_ROWS, FACTOR_PLACE, BASIS = factor_rows()


def tables():
    laplace = 2.0 * np.eye(SIDE) - np.roll(np.eye(SIDE), 1, 0) - np.roll(np.eye(SIDE), -1, 0)
    norms = np.sum(BASIS**2, 1)
    eigen_y = np.sum((BASIS @ laplace) * BASIS, 1) / norms
    points = np.arange(SIDE)
    eigen_z = 2.0 - 2.0 * np.cos(2.0 * math.pi * points / SIDE)
    mu = 1.0 / SIDE**2 + eigen_y[:, None] + eigen_z[None, :]
    ratio = 1.0 / (1.0 + mu / 2.0 + np.sqrt(mu + mu**2 / 4.0))
    scale = 1.0 / SIDE / (1.0 / ratio - ratio) / norms[:, None] / SIDE
    ratio = ratio.reshape(TILES, LANES)
    scale = scale.reshape(TILES, LANES)
    angle = 2.0 * math.pi * (points[:, None] * points[None, :] % SIDE) / SIDE
    along_z = np.cos(angle) + np.sin(angle)
    matrix = np.kron(np.array([[1.0, 1.0], [1.0, -1.0]]), along_z)
    high = matrix.astype(np.float32).astype(ml_dtypes.bfloat16)
    low = (matrix - high.astype(np.float64)).astype(ml_dtypes.bfloat16)
    row = np.concatenate([high, low], 1)
    weights = np.concatenate([row, row], 0)
    plain = np.stack([ratio, scale, ratio**32, 1.0 / (1.0 - ratio**64)])
    factors = np.repeat(FACTOR_ROWS[:, None, :], 8, 1)
    table = np.concatenate([factors, plain.reshape(-1, 8, LANES)], 0)
    return weights, table.astype(np.float32)


WEIGHTS, TABLE = tables()
assert len(FACTOR_ROWS) == FACTORS


def kernel_factors(table_ref):
    lane = lax.broadcasted_iota(jnp.int32, (8, LANES), 1)
    upper = lane >= SIDE

    def fetch(size, t):
        at = FACTOR_PLACE[(size, t)]
        return table_ref[at], table_ref[at + 1]

    return Factors(fetch, lambda a, b: jnp.where(upper, b, a))


def plain(table_ref, kind, group):
    return table_ref[FACTORS + GROUPS * kind + group]


def lanes_of(t):
    return pl.ds(t * LANES, LANES)


def transform_rows(values, weights):
    high = values.astype(jnp.bfloat16)
    low = (values - high.astype(jnp.float32)).astype(jnp.bfloat16)
    both = jnp.concatenate([high, low], 1)
    out = jnp.dot(both, weights, preferred_element_type=jnp.float32)
    return out[:, :LANES] + out[:, LANES:]


def pair_rows(ints_ref, slot):
    groups = lax.axis_size("band")
    below = lax.axis_index("band") + groups - 1
    first = ints_ref[2 * slot]
    partner = ints_ref[2 * slot + 1]
    alive = slot < ints_ref[8]
    hop = lax.rem(partner // 2 - lax.rem(below, groups) + groups, groups)
    second = 2 * hop + lax.rem(partner, 2)
    return jnp.where(alive, first, 0), jnp.where(alive, second, 0), alive


def for_slots(ints_ref, run):
    band = lax.axis_index("band")
    ends = (band == 0) | (band == lax.axis_size("band") - 1)
    count = jnp.where(ends, ints_ref[8], 4)
    pl.when(count == 1)(lambda: run((0,)))
    pl.when((count == 2) | (count == 3))(lambda: run((0, 1)))
    pl.when(count == 3)(lambda: run((2,)))
    pl.when(count >= 4)(lambda: run((0, 1, 2, 3)))


def cross_at():
    return 4 * lax.rem(lax.axis_index("band"), 2)


def pack_kernel(pairs_ref, count_ref, ints_ref):
    for n in range(4):
        ints_ref[2 * n] = pairs_ref[0, n, 0]
        ints_ref[2 * n + 1] = pairs_ref[0, n, 1]
    ints_ref[8] = count_ref[0]


def prepare_kernel(
    own_ref, weight_ref, table_ref,
    window, result, weights, table, sems,
):
    copies = [
        pltpu.make_async_copy(own_ref, window.at[pl.ds(2, 2)], sems.at[0]),
        pltpu.make_async_copy(weight_ref, weights, sems.at[1]),
        pltpu.make_async_copy(table_ref, table, sems.at[2]),
    ]
    for copy in copies:
        copy.start()
    result[...] = jnp.zeros_like(result)
    for copy in copies:
        copy.wait()


def forward_kernel(
    ints_ref, cross_ref, mate_ref, window_ref, weights, table,
    local_ref, edge_ref, window,
    stage, sems,
):
    rows = window.shape[1]
    cross = cross_at()
    copies = []
    for o in range(rows // 8):
        span = pl.ds(8 * o, 8)
        copies.append([
            pltpu.make_async_copy(ref.at[:, span], window.at[pl.ds(at, 2), span], sems.at[n, o])
            for n, (ref, at) in enumerate(((mate_ref, 4 - cross), (cross_ref, cross)))
        ])
        for copy in copies[o]:
            copy.start()
    for pair in copies:
        for copy in pair:
            copy.wait()
    factors = kernel_factors(table)

    def along_y(slot):
        first, second, _ = pair_rows(ints_ref, slot)
        for o in range(rows // 8):
            values = []
            for t in range(TILES):
                left = window[first, pl.ds(8 * o, 8), lanes_of(t)]
                right = window[second, pl.ds(8 * o, 8), lanes_of(t)]
                values.append(left * right)
            values = real_forward(values, SIDE, factors)
            for t in range(TILES):
                stage[slot, pl.ds((o * TILES + t) * 8, 8)] = values[t]

    def along_zx(slot, g):
        parts = [
            stage[slot, pl.ds(x // 8 * TILES * 8 + g * 64 + x % 8, 8, stride=8)]
            for x in range(rows)
        ]
        spectrum = transform_rows(jnp.concatenate(parts, 0), weights[...])
        weight = jnp.where(pair_rows(ints_ref, slot)[2], 1.0, 0.0).astype(jnp.float32)
        ratio, scale = plain(table, 0, g), plain(table, 1, g) * weight
        values = [spectrum[8 * x : 8 * x + 8] * scale for x in range(rows)]
        ahead = values[0]
        sums = [ahead]
        for x in range(1, rows):
            ahead = ahead * ratio
            sums.append(ahead)
            ahead = ahead + values[x]
        behind = values[rows - 1]
        local_ref[slot, g, rows - 1] = sums[rows - 1] + behind
        for x in range(rows - 2, -1, -1):
            behind = behind * ratio + values[x]
            local_ref[slot, g, x] = (sums[x] + behind) if x else behind
        edge_ref[slot, 0, g] = ahead
        edge_ref[slot, 1, g] = behind

    def run(slots):
        along_y(slots[0])
        for slot in slots:
            if slot != slots[-1]:
                along_y(slot + 1)
            for g in range(GROUPS):
                along_zx(slot, g)

    for_slots(ints_ref, run)


def back_kernel(
    ints_ref, window, local_ref, edge_ref, other_ref, weights, table, zero_ref,
    cross_ref, mate_ref, own_ref, result,
    fields, sems,
):
    rows = window.shape[1]
    cross = cross_at()
    factors = kernel_factors(table)

    def along_xz(slot, g):
        ratio, whole, closing = [plain(table, kind, g) for kind in (0, 2, 3)]
        ahead = (other_ref[slot, 0, g] + whole * edge_ref[slot, 0, g]) * closing
        behind = (other_ref[slot, 1, g] + whole * edge_ref[slot, 1, g]) * closing
        behinds = []
        for x in range(rows):
            behind = behind * ratio
            behinds.append(behind)
        parts = []
        for x in range(rows):
            ahead = ahead * ratio
            parts.append(local_ref[slot, g, x] + (ahead + behinds[rows - 1 - x]))
        values = transform_rows(jnp.concatenate(parts, 0), weights[...])
        for x in range(rows):
            fields[slot, pl.ds(x * TILES + 8 * g, 8)] = values[8 * x : 8 * x + 8]

    def along_y(slot):
        first, second, _ = pair_rows(ints_ref, slot)
        for o in range(rows // 8):
            values = [
                fields[slot, pl.ds(8 * o * TILES + t, 8, stride=TILES)] for t in range(TILES)
            ]
            values = real_back(values, SIDE, factors)
            span = pl.ds(8 * o, 8)
            for begin_t in range(0, TILES, 8):
                new = []
                for t in range(begin_t, begin_t + 8):
                    left = window[first, span, lanes_of(t)]
                    right = window[second, span, lanes_of(t)]
                    new.append((
                        result[first, span, lanes_of(t)] + values[t] * right,
                        result[second, span, lanes_of(t)] + values[t] * left,
                    ))
                for t in range(begin_t, begin_t + 8):
                    result[first, span, lanes_of(t)] = new[t - begin_t][0]
                for t in range(begin_t, begin_t + 8):
                    result[second, span, lanes_of(t)] = new[t - begin_t][1]

    def run(slots):
        for g in range(GROUPS):
            along_xz(slots[0], g)
        for slot in slots:
            if slot != slots[-1]:
                for g in range(GROUPS):
                    along_xz(slot + 1, g)
            along_y(slot)

    for_slots(ints_ref, run)
    copies = [
        pltpu.make_async_copy(result.at[pl.ds(at, 2)], ref, sems.at[n])
        for n, (ref, at) in enumerate(((cross_ref, cross), (mate_ref, 4 - cross), (own_ref, 2)))
    ]
    for copy in copies:
        copy.start()
    for copy in copies:
        copy.wait()


ANY = pl.BlockSpec(memory_space=pl.ANY)
HBM = pl.BlockSpec(memory_space=pltpu.HBM)
VMEM = pl.BlockSpec(memory_space=pltpu.VMEM)
SMEM = pl.BlockSpec(memory_space=pltpu.SMEM)
LIMIT = pltpu.CompilerParams(vmem_limit_bytes=20 * 1024 * 1024)
COST = pl.CostEstimate(flops=0, bytes_accessed=12_000_000, transcendentals=0)


def pack(pair_list, pair_count):
    return pl.pallas_call(
        pack_kernel,
        out_shape=jax.ShapeDtypeStruct((9,), jnp.int32),
        in_specs=[SMEM, SMEM],
        out_specs=SMEM,
        name="pack",
    )(pair_list, pair_count)


def prepare(own):
    shape = (6,) + own.shape[1:]
    return pl.pallas_call(
        prepare_kernel,
        out_shape=(
            jax.ShapeDtypeStruct(shape, jnp.float32),
            jax.ShapeDtypeStruct(shape, jnp.float32),
            jax.ShapeDtypeStruct(WEIGHTS.shape, jnp.bfloat16),
            jax.ShapeDtypeStruct(TABLE.shape, jnp.float32),
        ),
        in_specs=[HBM, HBM, HBM],
        out_specs=(VMEM, VMEM, VMEM, VMEM),
        scratch_shapes=[pltpu.SemaphoreType.DMA((3,))],
        compiler_params=LIMIT,
        cost_estimate=COST,
        name="prepare",
    )(own, WEIGHTS, TABLE)


def forward(ints, cross, mate, window, weights, table):
    rows = window.shape[1]
    return pl.pallas_call(
        forward_kernel,
        out_shape=(
            jax.ShapeDtypeStruct((4, GROUPS, rows, 8, LANES), jnp.float32),
            jax.ShapeDtypeStruct((4, 2, GROUPS, 8, LANES), jnp.float32),
            jax.ShapeDtypeStruct((6, rows, SIDE * SIDE), jnp.float32),
        ),
        in_specs=[SMEM, ANY, ANY, VMEM, VMEM, VMEM],
        out_specs=(VMEM, VMEM, VMEM),
        input_output_aliases={3: 2},
        scratch_shapes=[
            pltpu.VMEM((4, rows * TILES, LANES), jnp.float32),
            pltpu.SemaphoreType.DMA((2, rows // 8)),
        ],
        compiler_params=LIMIT,
        cost_estimate=COST,
        name="forward",
    )(ints, cross, mate, window, weights, table)


def back(ints, window, local, edges, other, weights, table, result):
    rows = window.shape[1]
    block = jax.ShapeDtypeStruct((2, rows, SIDE * SIDE), jnp.float32)
    return pl.pallas_call(
        back_kernel,
        out_shape=(block, block, block, jax.ShapeDtypeStruct(result.shape, jnp.float32)),
        in_specs=[SMEM] + [VMEM] * 7,
        out_specs=(ANY, ANY, ANY, VMEM),
        input_output_aliases={7: 3},
        scratch_shapes=[
            pltpu.VMEM((4, rows * TILES, LANES), jnp.float32),
            pltpu.SemaphoreType.DMA((3,)),
        ],
        compiler_params=LIMIT,
        cost_estimate=COST,
        name="back",
    )(ints, window, local, edges, other, weights, table, result)


def moved(value, axis, target):
    count = lax.axis_size(axis)
    return lax.ppermute(value, axis, [(n, target(n) % count) for n in range(count)])


def to_mate(value):
    return moved(value, "band", lambda n: n ^ 1)


def to_cross(value):
    return moved(value, "band", lambda n: n + 1 if n % 2 else n - 1)


def to_next_other_slab(value):
    count = lax.axis_size("band")
    pairs = [(2 * n + g, 2 * ((n + 1) % count) + 1 - g) for n in range(count) for g in range(2)]
    return lax.ppermute(value, ("band", "grid"), pairs)


def on_device(orbitals, pair_list, pair_count):
    cross = to_cross(orbitals)
    mate = to_mate(orbitals)
    ints = to_next_other_slab(pack(pair_list, pair_count))
    window, result, weights, table = prepare(orbitals)
    local, edges, window = forward(ints, cross, mate, window, weights, table)
    other = moved(edges, "grid", lambda n: n + 1)
    cross, mate, own, _ = back(ints, window, local, edges, other, weights, table, result)
    return (own + to_cross(cross)) + to_mate(mate)


def solution(mesh):
    in_specs = (P("band", "grid", None), P("band", None, None), P("band"))
    out_specs = P("band", "grid", None)
    return jax.shard_map(
        on_device, mesh=mesh, in_specs=in_specs, out_specs=out_specs, check_vma=False
    )
```

```python
import functools
import math

import jax
import jax.numpy as jnp
import ml_dtypes
import numpy as np
from jax import lax
from jax.experimental import pallas as pl
from jax.experimental.pallas import tpu as pltpu
from jax.sharding import PartitionSpec as P

SIDE = 64
TILES = SIDE // 2
LANES = 2 * SIDE
GROUPS = TILES // 8
FACTORS = 36


class Factors:
    def __init__(self, fetch, swap):
        self.fetch = fetch
        self.swap = swap


def turn(re, im, c, s):
    return re * c + im * s, im * c - re * s


def turn_back(re, im, c, s):
    return re * c - im * s, im * c + re * s


def complex_forward(re, im, size, factors):
    tiles = size // 2
    if tiles == 1:
        return [re[0], im[0]]
    half = tiles // 2
    even_re = [re[t] + re[t + half] for t in range(half)]
    even_im = [im[t] + im[t + half] for t in range(half)]
    odd_re, odd_im = [], []
    for t in range(half):
        a, b = re[t] - re[t + half], im[t] - im[t + half]
        if size == 4:
            a, b = factors.swap(a, b), factors.swap(b, -a)
        else:
            a, b = turn(a, b, *factors.fetch(size, t))
        odd_re.append(a)
        odd_im.append(b)
    return complex_forward(even_re, even_im, size // 2, factors) + complex_forward(
        odd_re, odd_im, size // 2, factors
    )


def complex_back(parts, size, factors):
    tiles = size // 2
    if tiles == 1:
        return [parts[0]], [parts[1]]
    half = tiles // 2
    even_re, even_im = complex_back(parts[:tiles], size // 2, factors)
    odd_re, odd_im = complex_back(parts[tiles:], size // 2, factors)
    low_re, low_im, high_re, high_im = [], [], [], []
    for t in range(half):
        a, b = odd_re[t], odd_im[t]
        if size == 4:
            a, b = factors.swap(a, -b), factors.swap(b, a)
        else:
            a, b = turn_back(a, b, *factors.fetch(size, t))
        low_re.append(even_re[t] + a)
        low_im.append(even_im[t] + b)
        high_re.append(even_re[t] - a)
        high_im.append(even_im[t] - b)
    return low_re + high_re, low_im + high_im


def real_forward(values, size, factors):
    tiles = size // 2
    if tiles == 1:
        return list(values)
    half = tiles // 2
    sums = [values[t] + values[t + half] for t in range(half)]
    rests = [values[t] - values[t + half] for t in range(half)]
    if size == 4:
        odd = rests
    else:
        quarter = half // 2
        re, im = [], []
        for t in range(quarter):
            a, b = turn(rests[t], -rests[t + quarter], *factors.fetch(size, t))
            re.append(a)
            im.append(b)
        odd = complex_forward(re, im, size // 4, factors)
    return real_forward(sums, size // 2, factors) + odd


def real_back(parts, size, factors):
    tiles = size // 2
    if tiles == 1:
        return list(parts)
    half = tiles // 2
    sums = real_back(parts[:half], size // 2, factors)
    if size == 4:
        rests = parts[half:]
    else:
        re, im = complex_back(parts[half:], size // 4, factors)
        quarter = half // 2
        low, high = [], []
        for t in range(quarter):
            a, b = turn_back(re[t], im[t], *factors.fetch(size, t))
            low.append(a)
            high.append(-b)
        rests = low + high
    return [sums[t] + rests[t] for t in range(half)] + [sums[t] - rests[t] for t in range(half)]


def factor_rows():
    rows, place, wanted = [], {}, []

    def note(size, t):
        if (size, t) not in wanted:
            wanted.append((size, t))
        angle = 2.0 * math.pi * (2 * t + np.arange(2)) / size
        return np.cos(angle)[:, None], np.sin(angle)[:, None]

    upper = np.array([False, True])[:, None]
    factors = Factors(note, lambda a, b: np.where(upper, b, a))
    unit = np.eye(SIDE).reshape(TILES, 2, SIDE)
    outs = real_forward([unit[t] for t in range(TILES)], SIDE, factors)
    outs = [np.stack([o[0] + o[1], o[0] - o[1]]) for o in outs]
    basis = np.concatenate(outs, 0)
    for size, t in wanted:
        angle = 2.0 * math.pi * (2 * t + np.repeat(np.arange(2), SIDE)) / size
        place[(size, t)] = len(rows)
        rows.append(np.cos(angle))
        rows.append(np.sin(angle))
    return np.stack(rows), place, basis


FACTOR_ROWS, FACTOR_PLACE, BASIS = factor_rows()


def tables():
    laplace = 2.0 * np.eye(SIDE) - np.roll(np.eye(SIDE), 1, 0) - np.roll(np.eye(SIDE), -1, 0)
    norms = np.sum(BASIS**2, 1)
    eigen_y = np.sum((BASIS @ laplace) * BASIS, 1) / norms
    points = np.arange(SIDE)
    eigen_z = 2.0 - 2.0 * np.cos(2.0 * math.pi * points / SIDE)
    mu = 1.0 / SIDE**2 + eigen_y[:, None] + eigen_z[None, :]
    ratio = 1.0 / (1.0 + mu / 2.0 + np.sqrt(mu + mu**2 / 4.0))
    scale = 1.0 / SIDE / (1.0 / ratio - ratio) / norms[:, None] / SIDE
    ratio = ratio.reshape(TILES, LANES)
    scale = scale.reshape(TILES, LANES)
    angle = 2.0 * math.pi * (points[:, None] * points[None, :] % SIDE) / SIDE
    along_z = np.cos(angle) + np.sin(angle)
    matrix = np.kron(np.array([[1.0, 1.0], [1.0, -1.0]]), along_z)
    high = matrix.astype(np.float32).astype(ml_dtypes.bfloat16)
    low = (matrix - high.astype(np.float64)).astype(ml_dtypes.bfloat16)
    row = np.concatenate([high, low], 1)
    weights = np.concatenate([row, row], 0)
    plain = np.stack([ratio, scale, ratio**32, 1.0 / (1.0 - ratio**64)])
    factors = np.repeat(FACTOR_ROWS[:, None, :], 8, 1)
    table = np.concatenate([factors, plain.reshape(-1, 8, LANES)], 0)
    return weights, table.astype(np.float32)


WEIGHTS, TABLE = tables()
assert len(FACTOR_ROWS) == FACTORS


def kernel_factors(table_ref):
    lane = lax.broadcasted_iota(jnp.int32, (8, LANES), 1)
    upper = lane >= SIDE

    def fetch(size, t):
        at = FACTOR_PLACE[(size, t)]
        return table_ref[at], table_ref[at + 1]

    return Factors(fetch, lambda a, b: jnp.where(upper, b, a))


def plain(table_ref, kind, group):
    return table_ref[FACTORS + GROUPS * kind + group]


def lanes_of(t):
    return pl.ds(t * LANES, LANES)


def transform_rows(values, weights):
    high = values.astype(jnp.bfloat16)
    low = (values - high.astype(jnp.float32)).astype(jnp.bfloat16)
    both = jnp.concatenate([high, low], 1)
    out = jnp.dot(both, weights, preferred_element_type=jnp.float32)
    return out[:, :LANES] + out[:, LANES:]


def pair_rows(ints_ref, slot):
    groups = lax.axis_size("band")
    below = lax.axis_index("band") + groups - 1
    first = ints_ref[2 * slot]
    partner = ints_ref[2 * slot + 1]
    alive = slot < ints_ref[8]
    hop = lax.rem(partner // 2 - lax.rem(below, groups) + groups, groups)
    second = 2 * hop + lax.rem(partner, 2)
    return jnp.where(alive, first, 0), jnp.where(alive, second, 0), alive


def for_slots(ints_ref, run):
    band = lax.axis_index("band")
    ends = (band == 0) | (band == lax.axis_size("band") - 1)
    count = jnp.where(ends, ints_ref[8], 4)
    pl.when(count == 1)(lambda: run((0,)))
    pl.when((count == 2) | (count == 3))(lambda: run((0, 1)))
    pl.when(count == 3)(lambda: run((2,)))
    pl.when(count >= 4)(lambda: run((0, 1, 2, 3)))


def cross_at():
    return 4 * lax.rem(lax.axis_index("band"), 2)


def pack_kernel(pairs_ref, count_ref, ints_ref):
    for n in range(4):
        ints_ref[2 * n] = pairs_ref[0, n, 0]
        ints_ref[2 * n + 1] = pairs_ref[0, n, 1]
    ints_ref[8] = count_ref[0]


def prepare_kernel(
    own_ref, weight_ref, table_ref,
    window, result, weights, table, sems,
):
    copies = [
        pltpu.make_async_copy(own_ref, window.at[pl.ds(2, 2)], sems.at[0]),
        pltpu.make_async_copy(weight_ref, weights, sems.at[1]),
        pltpu.make_async_copy(table_ref, table, sems.at[2]),
    ]
    for copy in copies:
        copy.start()
    result[...] = jnp.zeros_like(result)
    for copy in copies:
        copy.wait()


def forward_kernel(
    ints_ref, cross_ref, mate_ref, window_ref, weights, table,
    local_ref, edge_ref, window,
    stage, sems,
):
    rows = window.shape[1]
    cross = cross_at()
    copies = []
    for o in range(rows // 8):
        span = pl.ds(8 * o, 8)
        copies.append([
            pltpu.make_async_copy(ref.at[:, span], window.at[pl.ds(at, 2), span], sems.at[n, o])
            for n, (ref, at) in enumerate(((mate_ref, 4 - cross), (cross_ref, cross)))
        ])
        for copy in copies[o]:
            copy.start()
    for pair in copies:
        for copy in pair:
            copy.wait()
    factors = kernel_factors(table)

    def along_y(slot):
        first, second, _ = pair_rows(ints_ref, slot)
        for o in range(rows // 8):
            values = []
            for t in range(TILES):
                left = window[first, pl.ds(8 * o, 8), lanes_of(t)]
                right = window[second, pl.ds(8 * o, 8), lanes_of(t)]
                values.append(left * right)
            values = real_forward(values, SIDE, factors)
            for t in range(TILES):
                stage[slot, pl.ds((o * TILES + t) * 8, 8)] = values[t]

    def along_zx(slot, g):
        parts = [
            stage[slot, pl.ds(x // 8 * TILES * 8 + g * 64 + x % 8, 8, stride=8)]
            for x in range(rows)
        ]
        spectrum = transform_rows(jnp.concatenate(parts, 0), weights[...])
        weight = jnp.where(pair_rows(ints_ref, slot)[2], 1.0, 0.0).astype(jnp.float32)
        ratio, scale = plain(table, 0, g), plain(table, 1, g) * weight
        values = [spectrum[8 * x : 8 * x + 8] * scale for x in range(rows)]
        ahead = values[0]
        sums = [ahead]
        for x in range(1, rows):
            ahead = ahead * ratio
            sums.append(ahead)
            ahead = ahead + values[x]
        behind = values[rows - 1]
        local_ref[slot, g, rows - 1] = sums[rows - 1] + behind
        for x in range(rows - 2, -1, -1):
            behind = behind * ratio + values[x]
            local_ref[slot, g, x] = (sums[x] + behind) if x else behind
        edge_ref[slot, 0, g] = ahead
        edge_ref[slot, 1, g] = behind

    def run(slots):
        along_y(slots[0])
        for slot in slots:
            if slot != slots[-1]:
                along_y(slot + 1)
            for g in range(GROUPS):
                along_zx(slot, g)

    for_slots(ints_ref, run)


def back_kernel(
    ints_ref, window, local_ref, edge_ref, other_ref, weights, table, zero_ref,
    cross_ref, mate_ref, own_ref, result,
    fields, sems,
):
    rows = window.shape[1]
    cross = cross_at()
    factors = kernel_factors(table)

    def along_xz(slot, g):
        ratio, whole, closing = [plain(table, kind, g) for kind in (0, 2, 3)]
        ahead = (other_ref[slot, 0, g] + whole * edge_ref[slot, 0, g]) * closing
        behind = (other_ref[slot, 1, g] + whole * edge_ref[slot, 1, g]) * closing
        behinds = []
        for x in range(rows):
            behind = behind * ratio
            behinds.append(behind)
        parts = []
        for x in range(rows):
            ahead = ahead * ratio
            parts.append(local_ref[slot, g, x] + (ahead + behinds[rows - 1 - x]))
        values = transform_rows(jnp.concatenate(parts, 0), weights[...])
        for x in range(rows):
            fields[slot, pl.ds(x * TILES + 8 * g, 8)] = values[8 * x : 8 * x + 8]

    def along_y(slot):
        first, second, _ = pair_rows(ints_ref, slot)
        for o in range(rows // 8):
            values = [
                fields[slot, pl.ds(8 * o * TILES + t, 8, stride=TILES)] for t in range(TILES)
            ]
            values = real_back(values, SIDE, factors)
            span = pl.ds(8 * o, 8)
            for begin_t in range(0, TILES, 8):
                new = []
                for t in range(begin_t, begin_t + 8):
                    left = window[first, span, lanes_of(t)]
                    right = window[second, span, lanes_of(t)]
                    new.append((
                        result[first, span, lanes_of(t)] + values[t] * right,
                        result[second, span, lanes_of(t)] + values[t] * left,
                    ))
                for t in range(begin_t, begin_t + 8):
                    result[first, span, lanes_of(t)] = new[t - begin_t][0]
                for t in range(begin_t, begin_t + 8):
                    result[second, span, lanes_of(t)] = new[t - begin_t][1]

    def run(slots):
        for g in range(GROUPS):
            along_xz(slots[0], g)
        for slot in slots:
            if slot != slots[-1]:
                for g in range(GROUPS):
                    along_xz(slot + 1, g)
            along_y(slot)

    for_slots(ints_ref, run)
    copies = [
        pltpu.make_async_copy(result.at[pl.ds(at, 2)], ref, sems.at[n])
        for n, (ref, at) in enumerate(((cross_ref, cross), (mate_ref, 4 - cross), (own_ref, 2)))
    ]
    for copy in copies:
        copy.start()
    for copy in copies:
        copy.wait()


ANY = pl.BlockSpec(memory_space=pl.ANY)
HBM = pl.BlockSpec(memory_space=pltpu.HBM)
VMEM = pl.BlockSpec(memory_space=pltpu.VMEM)
SMEM = pl.BlockSpec(memory_space=pltpu.SMEM)
LIMIT = pltpu.CompilerParams(vmem_limit_bytes=20 * 1024 * 1024)
COST = pl.CostEstimate(flops=0, bytes_accessed=12_000_000, transcendentals=0)


def pack(pair_list, pair_count):
    return pl.pallas_call(
        pack_kernel,
        out_shape=jax.ShapeDtypeStruct((9,), jnp.int32),
        in_specs=[SMEM, SMEM],
        out_specs=SMEM,
        name="pack",
    )(pair_list, pair_count)


def prepare(own):
    shape = (6,) + own.shape[1:]
    return pl.pallas_call(
        prepare_kernel,
        out_shape=(
            jax.ShapeDtypeStruct(shape, jnp.float32),
            jax.ShapeDtypeStruct(shape, jnp.float32),
            jax.ShapeDtypeStruct(WEIGHTS.shape, jnp.bfloat16),
            jax.ShapeDtypeStruct(TABLE.shape, jnp.float32),
        ),
        in_specs=[HBM, HBM, HBM],
        out_specs=(VMEM, VMEM, VMEM, VMEM),
        scratch_shapes=[pltpu.SemaphoreType.DMA((3,))],
        compiler_params=LIMIT,
        cost_estimate=COST,
        name="prepare",
    )(own, WEIGHTS, TABLE)


def forward(ints, cross, mate, window, weights, table):
    rows = window.shape[1]
    return pl.pallas_call(
        forward_kernel,
        out_shape=(
            jax.ShapeDtypeStruct((4, GROUPS, rows, 8, LANES), jnp.float32),
            jax.ShapeDtypeStruct((4, 2, GROUPS, 8, LANES), jnp.float32),
            jax.ShapeDtypeStruct((6, rows, SIDE * SIDE), jnp.float32),
        ),
        in_specs=[SMEM, ANY, ANY, VMEM, VMEM, VMEM],
        out_specs=(VMEM, VMEM, VMEM),
        input_output_aliases={3: 2},
        scratch_shapes=[
            pltpu.VMEM((4, rows * TILES, LANES), jnp.float32),
            pltpu.SemaphoreType.DMA((2, rows // 8)),
        ],
        compiler_params=LIMIT,
        cost_estimate=COST,
        name="forward",
    )(ints, cross, mate, window, weights, table)


def back(ints, window, local, edges, other, weights, table, result):
    rows = window.shape[1]
    block = jax.ShapeDtypeStruct((2, rows, SIDE * SIDE), jnp.float32)
    return pl.pallas_call(
        back_kernel,
        out_shape=(block, block, block, jax.ShapeDtypeStruct(result.shape, jnp.float32)),
        in_specs=[SMEM] + [VMEM] * 7,
        out_specs=(ANY, ANY, ANY, VMEM),
        input_output_aliases={7: 3},
        scratch_shapes=[
            pltpu.VMEM((4, rows * TILES, LANES), jnp.float32),
            pltpu.SemaphoreType.DMA((3,)),
        ],
        compiler_params=LIMIT,
        cost_estimate=COST,
        name="back",
    )(ints, window, local, edges, other, weights, table, result)


def finish_kernel(own_ref, cross_ref, mate_ref, out_ref, total, sems):
    copies = []
    for n in range(2):
        for o in range(total.shape[1] // 8):
            span = pl.ds(8 * o, 8)
            total[n, span] = (own_ref[n, span] + cross_ref[n, span]) + mate_ref[n, span]
            copies.append(pltpu.make_async_copy(
                total.at[n, span], out_ref.at[n, span], sems.at[n, o]
            ))
            copies[-1].start()
    for copy in copies:
        copy.wait()


def finish(own, cross, mate):
    return pl.pallas_call(
        finish_kernel,
        out_shape=jax.ShapeDtypeStruct(own.shape, jnp.float32),
        in_specs=[VMEM, VMEM, VMEM],
        out_specs=HBM,
        scratch_shapes=[
            pltpu.VMEM(own.shape, jnp.float32),
            pltpu.SemaphoreType.DMA((2, own.shape[1] // 8)),
        ],
        compiler_params=LIMIT,
        name="finish",
    )(own, cross, mate)


def moved(value, axis, target):
    count = lax.axis_size(axis)
    return lax.ppermute(value, axis, [(n, target(n) % count) for n in range(count)])


def to_mate(value):
    return moved(value, "band", lambda n: n ^ 1)


def to_cross(value):
    return moved(value, "band", lambda n: n + 1 if n % 2 else n - 1)


def to_next_other_slab(value):
    count = lax.axis_size("band")
    pairs = [(2 * n + g, 2 * ((n + 1) % count) + 1 - g) for n in range(count) for g in range(2)]
    return lax.ppermute(value, ("band", "grid"), pairs)


def on_device(orbitals, pair_list, pair_count):
    cross = to_cross(orbitals)
    mate = to_mate(orbitals)
    ints = to_next_other_slab(pack(pair_list, pair_count))
    window, result, weights, table = prepare(orbitals)
    local, edges, window = forward(ints, cross, mate, window, weights, table)
    other = moved(edges, "grid", lambda n: n + 1)
    cross, mate, own, _ = back(ints, window, local, edges, other, weights, table, result)
    return finish(own, to_cross(cross), to_mate(mate))


def solution(mesh):
    in_specs = (P("band", "grid", None), P("band", None, None), P("band"))
    out_specs = P("band", "grid", None)
    return jax.shard_map(
        on_device, mesh=mesh, in_specs=in_specs, out_specs=out_specs, check_vma=False
    )
```
